32 devices in a mesh: context: 8 (over z, x), dp: 4 (over y, core).
Axes of the slice: x: 2, y: 2, z: 4, core: 2. Of those that a mesh axis runs over, the one named last changes fastest.
Arguments:
- queries: bfloat16 [4, 1024, 1024], P('dp', 'context'), may hold values from -12 to 12
- key_states: bfloat16 [4, 1024, 128], P('dp', 'context'), may hold values from -12 to 12
- value_states: bfloat16 [4, 1024, 128], P('dp', 'context'), may hold values from -6 to 6
- attn_out: bfloat16 [4, 1024, 1024], P('dp', 'context'), may hold values from -6 to 6
- out_grad: bfloat16 [4, 1024, 1024], P('dp', 'context'), may hold values from -6 to 6
- activations: bfloat16 [4, 1024, 8192], P('dp', 'context'), may hold values from -6 to 6
- segment_ids: int32 [4, 1024], P('dp', 'context'), may hold values from 0 to 3, as said below
- span_order: int32 [16], replicated, may hold values from 0 to 15, as said below
- kv_weight: float32 [2, 8192, 128], P(None, ('context', 'dp')), may hold values from -40 to 40
- moment_one: float32 [2, 8192, 128], P(None, ('context', 'dp')), may hold values from -200 to 200
- moment_two: float32 [2, 8192, 128], P(None, ('context', 'dp')), may hold values from 2 to 20000
Outputs:
- query_grad: bfloat16 [4, 1024, 1024], P('dp', 'context')
- kv_grad: bfloat16 [4, 1024, 256], P('dp', 'context')
- new_weight: float32 [2, 8192, 128], P(None, ('context', 'dp'))
- new_moment_one: float32 [2, 8192, 128], P(None, ('context', 'dp'))
- new_moment_two: float32 [2, 8192, 128], P(None, ('context', 'dp'))
- trust_ratio: float32 [2], replicated
The draws below stay inside these ranges and needn't reach their ends.
Inputs may be any that keep to these rules, and one draw needn't show every extreme that they name: `span_order`: stored spans 2i and 2i+1 hold the sequence's spans p and 15 - p, each span exactly once. `segment_ids`: along positions the ids never fall; every sequence holds ids 0 to 3; the document of the last position holds 8 positions or more.
All inputs are finite; a program needn't handle non-finite values.
Results may differ from the reference program's by a relative error of at most 0.0055.
Values may be sent and summed in bfloat16 or wider, within the bound.
No kernel may reach another device: no remote copies, remote signals or barrier semaphores. Data moves between devices by JAX's collectives and lax.ppermute only.
A program may use at most 64 MiB of HBM per device.

```python
import jax
import jax.numpy as jnp
from jax import lax

D = 8192
HEADS = 8
HEAD_DIM = 128
SEQ_DEV = 128
SEQ_LEN = 1024
SEQS = 4
N_CONTEXT = 8


def paired_order(key):
    key = jax.random.fold_in(key, 11)
    lower = jax.random.permutation(key, N_CONTEXT).astype(jnp.int32)
    upper = (2 * N_CONTEXT - 1 - lower).astype(jnp.int32)
    return jnp.stack([lower, upper], axis=1).reshape(2 * N_CONTEXT)


def layout_row(order, position):
    half = SEQ_DEV // 2
    inverse = jnp.argsort(order, stable=True).astype(jnp.int32)
    return inverse[position // half] * half + position % half


def drawn_rows(key):
    order = paired_order(key)
    position = (SEQ_LEN - 1 - 2 * jnp.arange(4, dtype=jnp.int32)).astype(jnp.int32)
    own_rows = layout_row(order, position)
    before_rows = layout_row(order, position - 1)
    return (own_rows, before_rows)


def blend_rows(base, rows_at):
    current = base[:, rows_at, :]
    return base.at[:, rows_at, :].set(current)


def draw_span_order(key, part):
    return paired_order(key)


def draw_segment_ids(key, part):
    order = paired_order(key)
    key = jax.random.fold_in(key, 5)
    half = SEQ_DEV // 2
    layout = jnp.arange(SEQ_LEN, dtype=jnp.int32)
    position = order[layout // half] * half + layout % half

    def single(subkey):
        cut_points = jax.random.permutation(subkey, SEQ_LEN - 8)[:3].astype(jnp.int32) + 1
        return jnp.sum((position[:, None] >= cut_points[None, :]).astype(jnp.int32), axis=1)
    return jax.vmap(single)(jax.random.split(key, SEQS)).astype(jnp.int32)


def draw_queries(key, part):
    own_rows, before_rows = drawn_rows(key)
    key = jax.random.fold_in(key, 1)
    shape = (SEQS, SEQ_LEN, HEADS * HEAD_DIM)
    base = jnp.clip(jax.random.normal(key, shape, jnp.float32), -4.0, 4.0)
    return blend_rows(base, own_rows).astype(jnp.bfloat16)


def draw_key_states(key, part):
    own_rows, before_rows = drawn_rows(key)
    key = jax.random.fold_in(key, 2)
    shape = (SEQS, SEQ_LEN, HEAD_DIM)
    base = jnp.clip(jax.random.normal(key, shape, jnp.float32), -4.0, 4.0)
    base = blend_rows(base, own_rows)
    return blend_rows(base, before_rows).astype(jnp.bfloat16)


def scaled_field(key, factor):
    first, second = jax.random.split(key)
    level = jnp.arange(D, dtype=jnp.float32) / D
    row_scale = jnp.power(10.0, level)
    column_scale = jnp.power(10.0, jax.random.uniform(second, (2, 1, HEAD_DIM), jnp.float32))
    return (first, factor * row_scale[None, :, None] * column_scale)


def draw_kv_weight(key, part):
    key = jax.random.fold_in(key, 21)
    noise_key, scale = scaled_field(key, 0.1)
    noise = jnp.clip(jax.random.normal(noise_key, (2, D, HEAD_DIM), jnp.float32), -4.0, 4.0)
    return noise * scale


def draw_moment_one(key, part):
    key = jax.random.fold_in(key, 22)
    noise_key, scale = scaled_field(key, 0.5)
    noise = jnp.clip(jax.random.normal(noise_key, (2, D, HEAD_DIM), jnp.float32), -4.0, 4.0)
    return noise * scale


def draw_moment_two(key, part):
    key = jax.random.fold_in(key, 23)
    noise_key, scale = scaled_field(key, 20.0)
    spread = jax.random.uniform(noise_key, (2, D, HEAD_DIM), jnp.float32, -1.0, 1.0)
    return jnp.power(10.0, spread) * scale


def block_scale(own_key, extent, cuts, low, high):
    gain, own = 1.0, jax.random.fold_in(own_key, 6)
    for dim, blocks in cuts:
        heights = jnp.exp(jax.random.uniform(jax.random.fold_in(own, dim), (blocks,), jnp.float32, low / len(cuts), high / len(cuts)))
        gain = gain * jnp.repeat(heights, extent[dim] // blocks).reshape([-1 if axis == dim else 1 for axis in range(len(extent))])
    return gain


def gaussian(stream_key, shape, scale, most, cuts=(), held_as=jnp.bfloat16):
    values = jax.random.normal(stream_key, shape, jnp.float32) * scale
    if len(cuts) > 0:
        values = block_scale(stream_key, shape, cuts, -0.22, 0.18) * values
    return jnp.clip(values, min=-most, max=most).astype(held_as)


def setup_inputs(seed: int = 0) -> dict:
    streams_of = jax.random.split(jax.random.key(seed), 12)
    return {
        "queries": draw_queries(jax.random.fold_in(streams_of[11], 71), 0),
        "key_states": draw_key_states(jax.random.fold_in(streams_of[11], 71), 0),
        "value_states": gaussian(streams_of[2], (SEQS, SEQ_LEN, HEAD_DIM), 1.0, 6.0, ((0, 4), (1, 8))),
        "attn_out": gaussian(streams_of[3], (SEQS, SEQ_LEN, HEADS * HEAD_DIM), 1.0, 6.0, ((0, 4), (1, 8))),
        "out_grad": gaussian(streams_of[4], (SEQS, SEQ_LEN, HEADS * HEAD_DIM), 1.0, 6.0, ((0, 4), (1, 8))),
        "activations": gaussian(streams_of[5], (SEQS, SEQ_LEN, D), 1.0, 6.0, ((0, 4), (1, 8))),
        "segment_ids": draw_segment_ids(jax.random.fold_in(streams_of[11], 71), 0),
        "span_order": draw_span_order(jax.random.fold_in(streams_of[11], 71), 0),
        "kv_weight": draw_kv_weight(jax.random.fold_in(streams_of[11], 71), 0),
        "moment_one": draw_moment_one(jax.random.fold_in(streams_of[11], 71), 0),
        "moment_two": draw_moment_two(jax.random.fold_in(streams_of[11], 71), 0),
    }


beta_one = 0.9
beta_two = 0.999
epsilon = 1e-06
weight_decay = 0.01
learn_rate = 0.01

def layout_positions(span_order):
    half = SEQ_DEV // 2
    layout = jnp.arange(SEQ_LEN, dtype=jnp.int32)
    return span_order[layout // half] * half + layout % half

def rounded(values):
    return lax.optimization_barrier(values.astype(jnp.bfloat16)).astype(jnp.float32)

def one_sequence(position, queries, key_states, value_states, attn_out, out_grad, segment):
    score_scale = HEAD_DIM ** (-0.5)
    query_all = queries.astype(jnp.float32).reshape(SEQ_LEN, HEADS, HEAD_DIM)
    grad_all = out_grad.astype(jnp.float32).reshape(SEQ_LEN, HEADS, HEAD_DIM)
    output_all = attn_out.astype(jnp.float32).reshape(SEQ_LEN, HEADS, HEAD_DIM)
    delta_all = lax.optimization_barrier(jnp.sum(grad_all * output_all, axis=2))
    key_float = key_states.astype(jnp.float32)
    value_float = value_states.astype(jnp.float32)

    def query_block_step(running, first_row):
        query_block = lax.dynamic_slice_in_dim(query_all, first_row, SEQ_DEV, 0)
        grad_block = lax.dynamic_slice_in_dim(grad_all, first_row, SEQ_DEV, 0)
        delta_block = lax.dynamic_slice_in_dim(delta_all, first_row, SEQ_DEV, 0)
        query_place = lax.dynamic_slice_in_dim(position, first_row, SEQ_DEV, 0)
        query_segment = lax.dynamic_slice_in_dim(segment, first_row, SEQ_DEV, 0)
        visible = (position[None, :] <= query_place[:, None]) & (segment[None, :] == query_segment[:, None])
        visible = visible[:, None, :]
        scores = jnp.einsum('qhd,kd->qhk', query_block, key_float) * score_scale
        masked = jnp.where(visible, scores, -jnp.inf)
        row_top = lax.optimization_barrier(jnp.max(masked, axis=2, keepdims=True))
        log_total = row_top + jnp.log(lax.optimization_barrier(jnp.sum(jnp.exp(masked - row_top), axis=2, keepdims=True)))
        probs = jnp.where(visible, jnp.exp(scores - log_total), 0.0)
        prob_grad = jnp.einsum('qhd,kd->qhk', grad_block, value_float)
        score_grad = rounded(score_scale * probs * (prob_grad - delta_block[:, :, None]))
        query_grad = jnp.einsum('qhk,kd->qhd', score_grad, key_float)
        key_grad = jnp.einsum('qhk,qhd->kd', score_grad, query_block)
        value_grad = jnp.einsum('qhk,qhd->kd', rounded(probs), grad_block)
        running = running + jnp.concatenate([key_grad, value_grad], axis=1)
        return (running, query_grad.reshape(SEQ_DEV, HEADS * HEAD_DIM).astype(jnp.bfloat16))
    starts = jnp.arange(0, SEQ_LEN, SEQ_DEV, dtype=jnp.int32)
    initial = jnp.zeros((SEQ_LEN, 2 * HEAD_DIM), jnp.float32)
    kv_float, query_grads = lax.scan(query_block_step, initial, starts)
    return (kv_float.astype(jnp.bfloat16), query_grads.reshape(SEQ_LEN, HEADS * HEAD_DIM))

def reference(queries, key_states, value_states, attn_out, out_grad, activations, segment_ids, span_order, kv_weight, moment_one, moment_two):
    position = layout_positions(span_order)
    kv_list = []
    query_list = []
    gradient = jnp.zeros((D, 2 * HEAD_DIM), jnp.float32)
    for sequence in range(SEQS):
        kv_low, query_grad = one_sequence(position, queries[sequence], key_states[sequence], value_states[sequence], attn_out[sequence], out_grad[sequence], segment_ids[sequence])
        kv_list.append(kv_low)
        query_list.append(query_grad)
        gradient = gradient + lax.dot_general(activations[sequence], kv_low, (((0,), (0,)), ((), ())), preferred_element_type=jnp.float32)
    gradient = jnp.stack([gradient[:, :HEAD_DIM], gradient[:, HEAD_DIM:]])
    new_one = beta_one * moment_one + (1.0 - beta_one) * gradient
    new_two = beta_two * moment_two + (1.0 - beta_two) * gradient * gradient
    update = new_one / (jnp.sqrt(new_two) + epsilon) + weight_decay * kv_weight
    weight_norm = jnp.sqrt(lax.optimization_barrier(jnp.sum(kv_weight * kv_weight, axis=(1, 2))))
    update_norm = jnp.sqrt(lax.optimization_barrier(jnp.sum(update * update, axis=(1, 2))))
    trust_ratio = weight_norm / (update_norm + epsilon)
    new_weight = kv_weight - learn_rate * trust_ratio[:, None, None] * update
    return (jnp.stack(query_list), jnp.stack(kv_list), new_weight, new_one, new_two, trust_ratio)
```

```python
import functools

import jax
import jax.numpy as jnp
from jax import lax
from jax.experimental import pallas as pl
from jax.experimental.pallas import tpu as pltpu
from jax.sharding import PartitionSpec as P

beta_one = 0.9
beta_two = 0.999
epsilon = 1e-06
weight_decay = 0.01
learn_rate = 0.01
LOG2E = 1.4426950408889634
VMEM_LIMIT = 40 * 1024 * 1024
HIDDEN = -1e30
ID_ROWS = 16


AXES = ("plane", "across", "dp")


def xor_permute(value, offset, total):
    return lax.ppermute(value, AXES, [(i, i ^ offset) for i in range(total)])


def local_call(kernel, name, out_shape, in_specs, scratch=(), out_specs=None, **cost):
    vmem = pl.BlockSpec(memory_space=pltpu.VMEM)
    return pl.pallas_call(
        kernel,
        out_shape=out_shape,
        in_specs=in_specs,
        out_specs=[vmem] * len(out_shape) if out_specs is None else out_specs,
        scratch_shapes=list(scratch),
        compiler_params=pltpu.CompilerParams(vmem_limit_bytes=VMEM_LIMIT),
        cost_estimate=pl.CostEstimate(
            flops=cost.get("flops", 0),
            bytes_accessed=cost.get("bytes_accessed", 0),
            transcendentals=cost.get("transcendentals", 0),
        ),
        name=name,
    )


VMEM = pl.BlockSpec(memory_space=pltpu.VMEM)
SMEM = pl.BlockSpec(memory_space=pltpu.SMEM)
ANYWHERE = pl.BlockSpec(memory_space=pl.ANY)


def pack_kernel(key_ref, value_ref, ids_ref, out_ref):
    rows, head_dim = key_ref.shape
    out_ref[:rows, :head_dim] = key_ref[...]
    out_ref[:rows, head_dim:] = value_ref[...]
    ids = ids_ref[...].astype(jnp.float32).astype(jnp.bfloat16)
    out_ref[rows:, :rows] = jnp.broadcast_to(ids, (ID_ROWS, rows))
    out_ref[rows:, rows:] = jnp.zeros((ID_ROWS, 2 * head_dim - rows), jnp.bfloat16)


def pack(keys, values, ids):
    rows, head_dim = keys.shape
    return local_call(
        pack_kernel,
        "pack_keys",
        [jax.ShapeDtypeStruct((rows + ID_ROWS, 2 * head_dim), jnp.bfloat16)],
        [VMEM] * 3,
        bytes_accessed=rows * head_dim * 8,
    )(keys, values, ids)[0]


def prepare_kernel(
    where_ref, span_ref, q_ref, o_ref, g_ref, q_all, g_all, delta_ref, base_ref, *, heads, half
):
    rows = q_ref.shape[0]
    head_dim = q_ref.shape[1] // heads
    me = where_ref[0]
    for head in range(heads):
        cols = slice(head * head_dim, (head + 1) * head_dim)
        at = pl.ds(head * rows, rows)
        grad = g_ref[:, cols]
        q_all[at, :] = q_ref[:, cols]
        g_all[at, :] = grad
        product = grad.astype(jnp.float32) * o_ref[:, cols].astype(jnp.float32)
        delta_ref[:, at] = jnp.sum(product.T, axis=0, keepdims=True)
    for piece in range(base_ref.shape[0] // 2):
        for part in range(2):
            start = span_ref[2 * (me ^ piece) + part] * half
            base_ref[2 * piece + part : 2 * piece + part + 1, :] = jnp.full(
                (1, rows), start, jnp.int32
            )


def prepare(where, span_order, queries, attn_out, out_grad, heads, count):
    rows, width = queries.shape
    head_dim = width // heads
    stacked = jax.ShapeDtypeStruct((heads * rows, head_dim), jnp.bfloat16)
    return local_call(
        functools.partial(prepare_kernel, heads=heads, half=rows // 2),
        "prepare_queries",
        [
            stacked,
            stacked,
            jax.ShapeDtypeStruct((1, heads * rows), jnp.float32),
            jax.ShapeDtypeStruct((2 * count, rows), jnp.int32),
        ],
        [SMEM, SMEM] + [VMEM] * 3,
        flops=2 * rows * width,
        bytes_accessed=10 * rows * width,
    )(where, span_order, queries, attn_out, out_grad)


def attention_kernel(q_all, g_all, delta_ref, base_ref, *refs, pieces, heads, tied):
    piece_refs = refs[:pieces]
    refs = refs[pieces + tied :]
    dq_ref = refs[0]
    chunk_refs = refs[1 : pieces + 1]
    k_all, v_all, k_t, bias, probs_t, grads_t = refs[pieces + 1 :]
    head_dim = q_all.shape[1]
    rows = q_all.shape[0] // heads
    half = rows // 2
    score_scale = head_dim ** (-0.5)

    for piece in range(pieces):
        at = pl.ds(piece * rows, rows)
        key = piece_refs[piece][:rows, :head_dim]
        k_all[at, :] = key
        v_all[at, :] = piece_refs[piece][:rows, head_dim:]
        k_t[:, at] = key.T

    segment_rows = [
        piece_refs[piece][rows : rows + 1, :rows].astype(jnp.float32) for piece in range(pieces)
    ]
    all_segments = jnp.concatenate(segment_rows, axis=0)
    mine = segment_rows[0]
    first = jnp.zeros((1, rows), jnp.int32)
    for document in range(1, 4):
        before = jnp.sum((all_segments < document).astype(jnp.int32))
        first = jnp.where(mine >= document, before, first)
    lane = lax.broadcasted_iota(jnp.int32, (1, rows), 1)
    place = jnp.where(lane < half, base_ref[0:1, :] + lane, base_ref[1:2, :] + lane - half)
    step = lax.broadcasted_iota(jnp.int32, (half, rows), 0)
    for part in range(2 * pieces):
        key_place = base_ref[part : part + 1, :] + step
        visible = (key_place >= first) & (key_place <= place)
        bias[pl.ds(part * half, half), :] = jnp.where(visible, 0.0, HIDDEN)

    group = 2
    width = group * rows
    for start in range(0, heads, group):
        at = pl.ds(start * rows, width)
        contract = (((1,), (1,)), ((), ()))
        scores = lax.dot_general(
            k_all[...], q_all[at, :], contract, preferred_element_type=jnp.float32
        )
        blocked = bias[...]
        scores = scores * (score_scale * LOG2E) + jnp.concatenate([blocked] * group, axis=1)
        top = jnp.max(scores, axis=0, keepdims=True)
        weights = jnp.exp2(scores - top)
        probs = weights * (1.0 / jnp.sum(weights, axis=0, keepdims=True))
        probs_t[:, at] = probs.astype(jnp.bfloat16)
        prob_grad = lax.dot_general(
            v_all[...], g_all[at, :], contract, preferred_element_type=jnp.float32
        )
        grads_t[:, at] = (score_scale * probs * (prob_grad - delta_ref[:, at])).astype(jnp.bfloat16)

    for piece in range(pieces):
        at = pl.ds(piece * rows, rows)
        key_grad = jnp.dot(grads_t[at, :], q_all[...], preferred_element_type=jnp.float32)
        value_grad = jnp.dot(probs_t[at, :], g_all[...], preferred_element_type=jnp.float32)
        kept = chunk_refs[piece].dtype
        chunk_refs[piece][:, :head_dim] = key_grad.astype(kept)
        chunk_refs[piece][:, head_dim:] = value_grad.astype(kept)
    for start in range(0, heads, group):
        at = pl.ds(start * rows, width)
        query_t = jnp.dot(k_t[...], grads_t[:, at], preferred_element_type=jnp.float32)
        for head in range(group):
            block = query_t[:, head * rows : (head + 1) * rows].T
            cols = pl.ds((start + head) * head_dim, head_dim)
            dq_ref[:, cols] = block.astype(jnp.bfloat16)


def attention(prepared, pieces, tied, heads):
    stacked, head_dim = prepared[0].shape
    rows = stacked // heads
    count = len(pieces)
    keys = count * rows
    work = stacked * keys
    chunk_types = [jnp.float32] + [jnp.bfloat16] * (count - 1)
    outs = local_call(
        functools.partial(attention_kernel, pieces=count, heads=heads, tied=len(tied)),
        "attention_backward",
        [jax.ShapeDtypeStruct((rows, heads * head_dim), jnp.bfloat16)]
        + [jax.ShapeDtypeStruct((rows, 2 * head_dim), kind) for kind in chunk_types],
        [VMEM] * (4 + count) + [ANYWHERE] * len(tied),
        [
            pltpu.VMEM((keys, head_dim), jnp.bfloat16),
            pltpu.VMEM((keys, head_dim), jnp.bfloat16),
            pltpu.VMEM((head_dim, keys), jnp.bfloat16),
            pltpu.VMEM((keys, rows), jnp.float32),
            pltpu.VMEM((keys, stacked), jnp.bfloat16),
            pltpu.VMEM((keys, stacked), jnp.bfloat16),
        ],
        flops=10 * work * head_dim,
        bytes_accessed=8 * stacked * head_dim,
        transcendentals=work,
    )(*prepared, *pieces, *tied)
    return outs[0], outs[1:]


def spread_kernel(where_ref, act_ref, *out_refs, planes, chips, cores, block):
    plane, chip, core = where_ref[1], where_ref[2], where_ref[3]
    for offset in range(chips):
        for other in range(cores):
            for step in range(planes):
                owner = ((plane ^ step) * chips + (chip ^ offset)) * cores + (core ^ other)
                to = (other * planes + step) * block
                out_refs[offset][:, to : to + block] = act_ref[
                    :, pl.ds(pl.multiple_of(owner * block, block), block)
                ]


def spread(where, activations, planes, chips, cores):
    rows, features = activations.shape
    part = jax.ShapeDtypeStruct((rows, features // chips), activations.dtype)
    block = features // (planes * chips * cores)
    return local_call(
        functools.partial(spread_kernel, planes=planes, chips=chips, cores=cores, block=block),
        "spread_activations",
        [part] * chips,
        [SMEM, VMEM],
        bytes_accessed=4 * rows * features,
    )(where, activations)


def total_kernel(*refs, count):
    total = refs[0][...]
    for ref in refs[1:count]:
        total = total + ref[...].astype(jnp.float32)
    refs[-1][...] = total.astype(jnp.bfloat16)


def total_kv(terms, tied):
    return local_call(
        functools.partial(total_kernel, count=len(terms)),
        "total_kv",
        [jax.ShapeDtypeStruct(terms[0].shape, jnp.bfloat16)],
        [VMEM] * len(terms) + [ANYWHERE] * len(tied),
        bytes_accessed=terms[0].size * 2 * (len(terms) + 2),
    )(*terms, *tied)[0]


def project_kernel(*refs, chips, half):
    act_refs, kv_refs = refs[:chips], refs[chips : 2 * chips]
    own_ref, other_ref, acts = refs[2 * chips :]
    rows = kv_refs[0].shape[0]
    for chip in range(chips):
        acts[pl.ds(chip * rows, rows), :] = act_refs[chip][...]
    kv_t = jnp.concatenate([ref[...].T for ref in kv_refs], axis=1)
    other_ref[...] = jnp.dot(
        kv_t, acts[:, half:], preferred_element_type=jnp.float32
    ).astype(jnp.bfloat16)
    own_ref[...] = jnp.dot(kv_t, acts[:, :half], preferred_element_type=jnp.float32)


def project(acts, kvs):
    chips = len(acts)
    rows, width = kvs[0].shape
    features = acts[0].shape[1]
    half = features // 2
    return local_call(
        functools.partial(project_kernel, chips=chips, half=half),
        "project",
        [
            jax.ShapeDtypeStruct((width, half), jnp.float32),
            jax.ShapeDtypeStruct((width, half), jnp.bfloat16),
        ],
        [VMEM] * (2 * chips),
        [pltpu.VMEM((chips * rows, features), jnp.bfloat16)],
        flops=2 * chips * rows * width * features,
        bytes_accessed=2 * chips * rows * (features + width),
    )(*acts, *kvs)


def combine_kernel(own_ref, other_ref, *out_refs):
    block = out_refs[0].shape[1]
    for step, out_ref in enumerate(out_refs):
        cols = slice(step * block, (step + 1) * block)
        total = own_ref[:, cols] + other_ref[:, cols].astype(jnp.float32)
        out_ref[...] = total.astype(out_ref.dtype)


def combine(own, other, planes):
    width, features = own.shape
    types = [jnp.float32] + [jnp.bfloat16] * (planes - 1)
    return local_call(
        combine_kernel,
        "combine_cores",
        [jax.ShapeDtypeStruct((width, features // planes), kind) for kind in types],
        [VMEM] * 2,
        bytes_accessed=8 * width * features,
    )(own, other)


def lamb_kernel(*refs, planes):
    grad_refs = refs[:planes]
    weight_ref, one_ref, two_ref = refs[planes : planes + 3]
    new_one_ref, new_two_ref, update_ref, sums_ref = refs[planes + 3 :]
    total = grad_refs[0][...]
    for ref in grad_refs[1:]:
        total = total + ref[...].astype(jnp.float32)
    gradient = total.T
    head_dim = weight_ref.shape[2]
    lane = lax.broadcasted_iota(jnp.int32, sums_ref.shape[1:], 1)
    sums = jnp.zeros(sums_ref.shape[1:], jnp.float32)
    for which in range(2):
        grad = gradient[:, which * head_dim : (which + 1) * head_dim]
        weight = weight_ref[which]
        new_one = beta_one * one_ref[which] + (1.0 - beta_one) * grad
        new_two = beta_two * two_ref[which] + (1.0 - beta_two) * grad * grad
        update = new_one / (jnp.sqrt(new_two) + epsilon) + weight_decay * weight
        new_one_ref[which] = new_one
        new_two_ref[which] = new_two
        update_ref[which] = update
        sums = sums + jnp.where(lane == which, jnp.sum(weight * weight), 0.0)
        sums = sums + jnp.where(lane == 2 + which, jnp.sum(update * update), 0.0)
    sums_ref[...] = jnp.broadcast_to(sums[None], sums_ref.shape)


def lamb(gradients, weight, one, two, total):
    state = jax.ShapeDtypeStruct(weight.shape, jnp.float32)
    return local_call(
        functools.partial(lamb_kernel, planes=len(gradients)),
        "lamb",
        [state, state, state, jax.ShapeDtypeStruct((total, 8, 128), jnp.float32)],
        [VMEM] * (len(gradients) + 3),
        bytes_accessed=28 * weight.size,
    )(*gradients, weight, one, two)


def finish_kernel(sums_ref, weight_ref, update_ref, new_weight_ref, ratio_ref):
    sums = jnp.sum(sums_ref[...], axis=0)[0:1, :]
    lane = lax.broadcasted_iota(jnp.int32, sums.shape, 1)

    def pick(which):
        return jnp.sum(jnp.where(lane == which, sums, 0.0), axis=1, keepdims=True)

    for which in range(2):
        ratio = jnp.sqrt(pick(which)) / (jnp.sqrt(pick(2 + which)) + epsilon)
        new_weight_ref[which] = weight_ref[which] - learn_rate * ratio * update_ref[which]
        ratio_ref[which] = ratio[0, 0]


def finish(sums, weight, update):
    return local_call(
        finish_kernel,
        "finish",
        [
            jax.ShapeDtypeStruct(weight.shape, jnp.float32),
            jax.ShapeDtypeStruct((2,), jnp.float32),
        ],
        [VMEM] * 3,
        out_specs=[VMEM, SMEM],
        bytes_accessed=12 * weight.size,
    )(sums, weight, update)


def on_device_small(
    queries,
    key_states,
    value_states,
    attn_out,
    out_grad,
    activations,
    segment_ids,
    span_order,
    kv_weight,
    moment_one,
    moment_two,
):
    cores = 2
    dp_count = lax.axis_size("dp")
    planes = lax.axis_size("plane")
    places = lax.axis_size("across") * dp_count
    chips = places // cores
    total = planes * places
    count = total // dp_count
    heads = queries.shape[2] // key_states.shape[2]
    linear = lax.axis_index(AXES)
    where = jnp.stack(
        [linear // dp_count, linear // places, linear % places // cores, linear % cores]
    ).astype(jnp.int32)

    own = pack(key_states[0], value_states[0], segment_ids)
    pieces = [own] + [xor_permute(own, m * dp_count, total) for m in range(1, count)]
    parts = spread(where, activations[0], planes, chips, cores)
    acts = [parts[0]] + [xor_permute(parts[m], m * cores, total) for m in range(1, chips)]
    prepared = prepare(where, span_order, queries[0], attn_out[0], out_grad[0], heads, count)

    query_grad, chunks = attention(prepared, pieces, acts[1:-1], heads)
    terms = [chunks[0]] + [xor_permute(chunks[m], m * dp_count, total) for m in range(1, count)]
    kv_low = total_kv(terms, acts[-1:])

    kvs = [kv_low] + [xor_permute(kv_low, m * cores, total) for m in range(1, chips)]
    partial, sent = project(acts, kvs)
    blocks = combine(partial, xor_permute(sent, 1, total), planes)
    gradients = [blocks[0]] + [xor_permute(blocks[m], m * places, total) for m in range(1, planes)]
    new_one, new_two, update, sums = lamb(gradients, kv_weight, moment_one, moment_two, total)
    sums = lax.all_to_all(sums, AXES, split_axis=0, concat_axis=0)
    new_weight, ratios = finish(sums, kv_weight, update)
    return (query_grad[None], kv_low[None], new_weight, new_one, new_two, ratios)


def layout_positions(span_order, first_row, row_count, half):
    layout = first_row + jnp.arange(row_count, dtype=jnp.int32)
    which = layout // half
    table = jnp.arange(span_order.shape[0], dtype=jnp.int32)
    picked = jnp.sum(jnp.where(which[:, None] == table[None, :], span_order[None, :], 0), axis=1)
    return picked * half + layout % half


def block_size(total_rows, query_rows):
    block_rows = total_rows
    while block_rows > 4 * query_rows and block_rows % 2 == 0:
        block_rows = block_rows // 2
    return block_rows


def on_device(
    queries,
    key_states,
    value_states,
    attn_out,
    out_grad,
    activations,
    segment_ids,
    span_order,
    kv_weight,
    moment_one,
    moment_two,
):
    device = lax.axis_index("context")
    query_rows = queries.shape[1]
    half = query_rows // 2
    head_dim = key_states.shape[2]
    heads = queries.shape[2] // head_dim
    score_scale = head_dim ** (-0.5)
    query_heads = queries[0].reshape(query_rows, heads, head_dim)
    grad_heads = out_grad[0].reshape(query_rows, heads, head_dim)
    output_heads = attn_out[0].reshape(query_rows, heads, head_dim)
    delta = jnp.sum(grad_heads.astype(jnp.float32) * output_heads.astype(jnp.float32), axis=2)
    query_place = layout_positions(span_order, device * query_rows, query_rows, half)
    query_segment = segment_ids[0]
    all_segments = lax.all_gather(segment_ids, "context", axis=1, tiled=True)[0]

    def visible_for(first_row, row_count):
        key_place = layout_positions(span_order, first_row, row_count, half)
        key_segment = lax.dynamic_slice_in_dim(all_segments, first_row, row_count, 0)
        visible = (key_place[None, :] <= query_place[:, None]) & (
            key_segment[None, :] == query_segment[:, None]
        )
        return visible[:, None, :]

    def score_block(key_block):
        return (
            jnp.einsum("qhd,kd->qhk", query_heads, key_block, preferred_element_type=jnp.float32)
            * score_scale
        )

    seq_length = query_rows * lax.axis_size("context")
    start_stats = (
        jnp.full((query_rows, heads), -1e30, jnp.float32),
        jnp.zeros((query_rows, heads), jnp.float32),
    )
    start_grads = (
        jnp.zeros((query_rows, heads, head_dim), jnp.float32),
        jnp.zeros((seq_length, 2 * head_dim), jnp.float32),
    )
    key_piece = lax.all_gather(key_states, "context", axis=1, tiled=True)
    value_piece = lax.all_gather(value_states, "context", axis=1, tiled=True)
    piece_rows = key_piece.shape[1]
    block_rows = block_size(piece_rows, query_rows)

    def stats_step(block_index, state):
        row_top, row_total = state
        offset = block_index * block_rows
        key_block = lax.dynamic_slice_in_dim(key_piece[0], offset, block_rows, 0)
        visible = visible_for(offset, block_rows)
        scores = score_block(key_block)
        masked = jnp.where(visible, scores, -1e30)
        new_top = jnp.maximum(row_top, jnp.max(masked, axis=2))
        weights = jnp.where(visible, jnp.exp(scores - new_top[:, :, None]), 0.0)
        return (new_top, row_total * jnp.exp(row_top - new_top) + jnp.sum(weights, axis=2))

    row_top, row_total = lax.fori_loop(0, piece_rows // block_rows, stats_step, start_stats)
    log_total = row_top + jnp.log(row_total)

    def grad_step(block_index, state):
        query_acc, kv_acc = state
        offset = block_index * block_rows
        key_block = lax.dynamic_slice_in_dim(key_piece[0], offset, block_rows, 0)
        value_block = lax.dynamic_slice_in_dim(value_piece[0], offset, block_rows, 0)
        visible = visible_for(offset, block_rows)
        probs = jnp.where(visible, jnp.exp(score_block(key_block) - log_total[:, :, None]), 0.0)
        prob_grad = jnp.einsum(
            "qhd,kd->qhk", grad_heads, value_block, preferred_element_type=jnp.float32
        )
        score_grad = (score_scale * probs * (prob_grad - delta[:, :, None])).astype(jnp.bfloat16)
        query_acc = query_acc + jnp.einsum(
            "qhk,kd->qhd", score_grad, key_block, preferred_element_type=jnp.float32
        )
        key_grad = jnp.einsum(
            "qhk,qhd->kd", score_grad, query_heads, preferred_element_type=jnp.float32
        )
        value_grad = jnp.einsum(
            "qhk,qhd->kd",
            probs.astype(jnp.bfloat16),
            grad_heads,
            preferred_element_type=jnp.float32,
        )
        current = lax.dynamic_slice_in_dim(kv_acc, offset, block_rows, 0)
        summed = current + jnp.concatenate([key_grad, value_grad], axis=1)
        return (query_acc, lax.dynamic_update_slice_in_dim(kv_acc, summed, offset, 0))

    query_acc, kv_acc = lax.fori_loop(0, piece_rows // block_rows, grad_step, start_grads)
    kv_summed = lax.psum_scatter(kv_acc, "context", scatter_dimension=0, tiled=True)
    kv_low = kv_summed.astype(jnp.bfloat16)
    feature_rows = activations[0]
    gradient = lax.psum_scatter(
        lax.dot_general(
            feature_rows, kv_low, (((0,), (0,)), ((), ())), preferred_element_type=jnp.float32
        ),
        ("context", "dp"),
        scatter_dimension=0,
        tiled=True,
    )
    gradient = jnp.stack([gradient[:, :head_dim], gradient[:, head_dim:]])
    new_one = beta_one * moment_one + (1.0 - beta_one) * gradient
    new_two = beta_two * moment_two + (1.0 - beta_two) * gradient * gradient
    update = new_one / (jnp.sqrt(new_two) + epsilon) + weight_decay * kv_weight
    weight_sums, update_sums = lax.psum(
        (jnp.sum(kv_weight * kv_weight, axis=(1, 2)), jnp.sum(update * update, axis=(1, 2))),
        ("context", "dp"),
    )
    trust_ratio = jnp.sqrt(weight_sums) / (jnp.sqrt(update_sums) + epsilon)
    new_weight = kv_weight - learn_rate * trust_ratio[:, None, None] * update
    query_grad = query_acc.reshape(query_rows, heads * head_dim).astype(jnp.bfloat16)
    return (query_grad[None], kv_low[None], new_weight, new_one, new_two, trust_ratio)


def solution(mesh):
    in_specs = (
        P("dp", "context", None),
        P("dp", "context", None),
        P("dp", "context", None),
        P("dp", "context", None),
        P("dp", "context", None),
        P("dp", "context", None),
        P("dp", "context"),
        P(),
        P(None, ("context", "dp"), None),
        P(None, ("context", "dp"), None),
        P(None, ("context", "dp"), None),
    )
    out_specs = (
        P("dp", "context", None),
        P("dp", "context", None),
        P(None, ("context", "dp"), None),
        P(None, ("context", "dp"), None),
        P(None, ("context", "dp"), None),
        P(),
    )
    if mesh.shape["context"] == 8 and mesh.shape["dp"] == 4:
        split = jax.sharding.Mesh(mesh.devices.reshape(4, 2, 4), AXES)
        context = AXES[:2]

        def renamed(specs):
            return tuple(
                P(*[
                    context if name == "context" else AXES if isinstance(name, tuple) else name
                    for name in spec
                ])
                for spec in specs
            )

        return jax.shard_map(
            on_device_small,
            mesh=split,
            in_specs=renamed(in_specs),
            out_specs=renamed(out_specs),
            check_vma=False,
        )
    return jax.shard_map(
        on_device, mesh=mesh, in_specs=in_specs, out_specs=out_specs, check_vma=False
    )
```

```python
import functools

import jax
import jax.numpy as jnp
from jax import lax
from jax.experimental import pallas as pl
from jax.experimental.pallas import tpu as pltpu
from jax.sharding import PartitionSpec as P

beta_one = 0.9
beta_two = 0.999
epsilon = 1e-06
weight_decay = 0.01
learn_rate = 0.01
LOG2E = 1.4426950408889634
VMEM_LIMIT = 40 * 1024 * 1024
VMEM_MOST = 60 * 1024 * 1024
HIDDEN = -1e30
ID_ROWS = 16


AXES = ("plane", "across", "dp")


def my_place():
    dp = lax.axis_index("dp")
    return lax.axis_index("plane"), lax.axis_index("across"), dp // 2, dp % 2


def xor_permute(value, offset, total):
    return lax.ppermute(value, AXES, [(i, i ^ offset) for i in range(total)])


def local_call(kernel, name, out_shape, in_specs, scratch=(), out_specs=None, limit=None, **cost):
    vmem = pl.BlockSpec(memory_space=pltpu.VMEM)
    return pl.pallas_call(
        kernel,
        out_shape=out_shape,
        in_specs=in_specs,
        out_specs=[vmem] * len(out_shape) if out_specs is None else out_specs,
        scratch_shapes=list(scratch),
        compiler_params=pltpu.CompilerParams(vmem_limit_bytes=limit or VMEM_LIMIT),
        cost_estimate=pl.CostEstimate(
            flops=cost.get("flops", 0),
            bytes_accessed=cost.get("bytes_accessed", 0),
            transcendentals=cost.get("transcendentals", 0),
        ),
        name=name,
    )


VMEM = pl.BlockSpec(memory_space=pltpu.VMEM)
SMEM = pl.BlockSpec(memory_space=pltpu.SMEM)
ANYWHERE = pl.BlockSpec(memory_space=pl.ANY)


def write_piece(key_ref, value_ref, ids_ref, out_ref):
    rows, head_dim = key_ref.shape
    out_ref[:rows, :head_dim] = key_ref[...]
    out_ref[:rows, head_dim:] = value_ref[...]
    ids = ids_ref[...].astype(jnp.float32).astype(jnp.bfloat16)
    out_ref[rows:, :rows] = jnp.broadcast_to(ids, (ID_ROWS, rows))
    out_ref[rows:, rows:] = jnp.zeros((ID_ROWS, 2 * head_dim - rows), jnp.bfloat16)


def pack_kernel(
    key_ref, value_ref, ids_ref, act_ref, out_ref, sent_ref, piece, ids, stage, sems, *, block
):
    rows, head_dim = key_ref.shape
    wide = 2 * block
    count = sent_ref.shape[1] // wide
    other = 1 - my_place()[2]
    small = [
        pltpu.make_async_copy(key_ref, piece.at[:rows, :head_dim], sems.at[2 * count]),
        pltpu.make_async_copy(value_ref, piece.at[:rows, head_dim:], sems.at[2 * count + 1]),
        pltpu.make_async_copy(ids_ref, ids, sems.at[2 * count + 2]),
    ]
    arriving, leaving = [], []
    for index in range(count):
        start = pl.multiple_of((2 * index + other) * wide, wide)
        to = pl.ds(index * wide, wide)
        arriving.append(
            pltpu.make_async_copy(
                act_ref.at[:, pl.ds(start, wide)], stage.at[:, to], sems.at[index]
            )
        )
        leaving.append(
            pltpu.make_async_copy(stage.at[:, to], sent_ref.at[:, to], sems.at[count + index])
        )
    for copy in small + arriving:
        copy.start()
    for copy in small:
        copy.wait()
    low = ids[...].astype(jnp.float32).astype(jnp.bfloat16)
    piece[rows:, :rows] = jnp.broadcast_to(low, (ID_ROWS, rows))
    piece[rows:, rows:] = jnp.zeros((ID_ROWS, 2 * head_dim - rows), jnp.bfloat16)
    result = pltpu.make_async_copy(piece, out_ref, sems.at[2 * count + 3])
    result.start()
    for here, there in zip(arriving, leaving):
        here.wait()
        there.start()
    for copy in leaving:
        copy.wait()
    result.wait()


def pack(keys, values, ids, activations, block):
    rows, head_dim = keys.shape
    half = activations.shape[1] // 2
    packed = (rows + ID_ROWS, 2 * head_dim)
    return local_call(
        functools.partial(pack_kernel, block=block),
        "pack",
        [
            jax.ShapeDtypeStruct(packed, jnp.bfloat16),
            jax.ShapeDtypeStruct((rows, half), jnp.bfloat16),
        ],
        [ANYWHERE] * 4,
        [
            pltpu.VMEM(packed, jnp.bfloat16),
            pltpu.VMEM(ids.shape, jnp.int32),
            pltpu.VMEM((rows, half), jnp.bfloat16),
            pltpu.SemaphoreType.DMA((half // block + 4,)),
        ],
        out_specs=[ANYWHERE] * 2,
        limit=VMEM_MOST,
        bytes_accessed=4 * rows * half,
    )(keys, values, ids, activations)


def prepare_kernel(
    span_ref,
    key_ref,
    value_ref,
    ids_ref,
    q_ref,
    o_ref,
    g_ref,
    piece_ref,
    q_all,
    g_all,
    delta_ref,
    base_ref,
    *,
    heads,
    half,
):
    write_piece(key_ref, value_ref, ids_ref, piece_ref)
    rows = q_ref.shape[0]
    head_dim = q_ref.shape[1] // heads
    plane, across, _, _ = my_place()
    me = 2 * plane + across
    for head in range(heads):
        cols = slice(head * head_dim, (head + 1) * head_dim)
        at = pl.ds(head * rows, rows)
        grad = g_ref[:, cols]
        q_all[at, :] = q_ref[:, cols]
        g_all[at, :] = grad
        product = grad.astype(jnp.float32) * o_ref[:, cols].astype(jnp.float32)
        delta_ref[:, at] = jnp.sum(product.T, axis=0, keepdims=True)
    for piece in range(base_ref.shape[0] // 2):
        for part in range(2):
            start = span_ref[2 * (me ^ piece) + part] * half
            base_ref[2 * piece + part : 2 * piece + part + 1, :] = jnp.full(
                (1, rows), start, jnp.int32
            )


def prepare(span_order, keys, values, ids, queries, attn_out, out_grad, heads, count):
    rows, width = queries.shape
    head_dim = width // heads
    stacked = jax.ShapeDtypeStruct((heads * rows, head_dim), jnp.bfloat16)
    return local_call(
        functools.partial(prepare_kernel, heads=heads, half=rows // 2),
        "prepare_queries",
        [
            jax.ShapeDtypeStruct((rows + ID_ROWS, 2 * head_dim), jnp.bfloat16),
            stacked,
            stacked,
            jax.ShapeDtypeStruct((1, heads * rows), jnp.float32),
            jax.ShapeDtypeStruct((2 * count, rows), jnp.int32),
        ],
        [SMEM] + [VMEM] * 6,
        flops=2 * rows * width,
        bytes_accessed=10 * rows * width,
    )(span_order, keys, values, ids, queries, attn_out, out_grad)


def attention_kernel(q_all, g_all, delta_ref, base_ref, *refs, pieces, heads):
    piece_refs = refs[:pieces]
    probs_t, grads_t, k_t, k_all, v_all, bias = refs[pieces:]
    head_dim = q_all.shape[1]
    rows = q_all.shape[0] // heads
    half = rows // 2
    score_scale = head_dim ** (-0.5)

    for piece in range(pieces):
        at = pl.ds(piece * rows, rows)
        key = piece_refs[piece][:rows, :head_dim]
        k_all[at, :] = key
        v_all[at, :] = piece_refs[piece][:rows, head_dim:]
        k_t[:, at] = key.T

    segment_rows = [
        piece_refs[piece][rows : rows + 1, :rows].astype(jnp.float32) for piece in range(pieces)
    ]
    all_segments = jnp.concatenate(segment_rows, axis=0)
    mine = segment_rows[0]
    first = jnp.zeros((1, rows), jnp.int32)
    for document in range(1, 4):
        before = jnp.sum((all_segments < document).astype(jnp.int32))
        first = jnp.where(mine >= document, before, first)
    lane = lax.broadcasted_iota(jnp.int32, (1, rows), 1)
    place = jnp.where(lane < half, base_ref[0:1, :] + lane, base_ref[1:2, :] + lane - half)
    step = lax.broadcasted_iota(jnp.int32, (half, rows), 0)
    for part in range(2 * pieces):
        key_place = base_ref[part : part + 1, :] + step
        visible = (key_place >= first) & (key_place <= place)
        bias[pl.ds(part * half, half), :] = jnp.where(visible, 0.0, HIDDEN)

    group = 2
    width = group * rows
    for start in range(0, heads, group):
        at = pl.ds(start * rows, width)
        contract = (((1,), (1,)), ((), ()))
        scores = lax.dot_general(
            k_all[...], q_all[at, :], contract, preferred_element_type=jnp.float32
        )
        blocked = bias[...]
        scores = scores * (score_scale * LOG2E) + jnp.concatenate([blocked] * group, axis=1)
        top = jnp.max(scores, axis=0, keepdims=True)
        weights = jnp.exp2(scores - top)
        probs = weights * (1.0 / jnp.sum(weights, axis=0, keepdims=True))
        probs_t[:, at] = probs.astype(jnp.bfloat16)
        prob_grad = lax.dot_general(
            v_all[...], g_all[at, :], contract, preferred_element_type=jnp.float32
        )
        grads_t[:, at] = (score_scale * probs * (prob_grad - delta_ref[:, at])).astype(jnp.bfloat16)


def attention(prepared, pieces, heads):
    stacked, head_dim = prepared[0].shape
    rows = stacked // heads
    keys = len(pieces) * rows
    work = stacked * keys
    square = jax.ShapeDtypeStruct((keys, stacked), jnp.bfloat16)
    return local_call(
        functools.partial(attention_kernel, pieces=len(pieces), heads=heads),
        "attention_scores",
        [square, square, jax.ShapeDtypeStruct((head_dim, keys), jnp.bfloat16)],
        [VMEM] * (4 + len(pieces)),
        [
            pltpu.VMEM((keys, head_dim), jnp.bfloat16),
            pltpu.VMEM((keys, head_dim), jnp.bfloat16),
            pltpu.VMEM((keys, rows), jnp.float32),
        ],
        flops=4 * work * head_dim,
        bytes_accessed=4 * work,
        transcendentals=work,
    )(*prepared, *pieces)


def terms_kernel(probs_t, grads_t, q_all, g_all, *refs, groups, rows):
    out_refs = refs[-len(groups) :]
    head_dim = q_all.shape[1]
    for out_ref, group in zip(out_refs, groups):
        for index, piece in enumerate(group):
            at = pl.ds(piece * rows, rows)
            to = pl.ds(index * rows, rows)
            key_grad = jnp.dot(grads_t[at, :], q_all[...], preferred_element_type=jnp.float32)
            value_grad = jnp.dot(probs_t[at, :], g_all[...], preferred_element_type=jnp.float32)
            out_ref[to, :head_dim] = key_grad.astype(out_ref.dtype)
            out_ref[to, head_dim:] = value_grad.astype(out_ref.dtype)


def kv_terms(probs_t, grads_t, q_all, g_all, tied, groups, kind, rows):
    keys, stacked = probs_t.shape
    head_dim = q_all.shape[1]
    return local_call(
        functools.partial(terms_kernel, groups=groups, rows=rows),
        "kv_terms",
        [jax.ShapeDtypeStruct((len(group) * rows, 2 * head_dim), kind) for group in groups],
        [VMEM] * 4 + [ANYWHERE] * len(tied),
        flops=2 * keys * stacked * head_dim,
        bytes_accessed=2 * keys * stacked,
    )(probs_t, grads_t, q_all, g_all, *tied)


def query_kernel(k_t, grads_t, dq_ref, mark_ref, *, heads):
    mark_ref[...] = jnp.zeros_like(mark_ref)
    head_dim = k_t.shape[0]
    rows = grads_t.shape[1] // heads
    group = 2
    for start in range(0, heads, group):
        at = pl.ds(start * rows, group * rows)
        query_t = jnp.dot(k_t[...], grads_t[:, at], preferred_element_type=jnp.float32)
        for head in range(group):
            block = query_t[:, head * rows : (head + 1) * rows].T
            cols = pl.ds((start + head) * head_dim, head_dim)
            dq_ref[:, cols] = block.astype(jnp.bfloat16)


def query_gradient(k_t, grads_t, heads):
    head_dim, keys = k_t.shape
    stacked = grads_t.shape[1]
    return local_call(
        functools.partial(query_kernel, heads=heads),
        "query_gradient",
        [
            jax.ShapeDtypeStruct((stacked // heads, heads * head_dim), jnp.bfloat16),
            jax.ShapeDtypeStruct((8, 128), jnp.float32),
        ],
        [VMEM] * 2,
        flops=2 * keys * stacked * head_dim,
        bytes_accessed=2 * keys * stacked,
    )(k_t, grads_t)


def chunk_groups(planes):
    return [
        [(core, across, step) for core in range(2) for across in range(2)]
        for step in reversed(range(planes))
    ]


def chunk_starts(place, offsets, block):
    core, across, step = offsets
    chip = (place[0] ^ step) * 2 + (place[1] ^ across)
    core = place[3] ^ core
    own = ((2 * chip + place[2]) * 2 + core) * block
    return pl.multiple_of(own, block), pl.multiple_of((2 * chip + core) * block, block)


def total_kernel(*refs, count):
    total = refs[0][...]
    for ref in refs[1:count]:
        total = total + ref[...].astype(jnp.float32)
    refs[-2][...] = total
    refs[-1][...] = total.astype(jnp.bfloat16)


def total_kv(terms, tied):
    return local_call(
        functools.partial(total_kernel, count=len(terms)),
        "total_kv",
        [jax.ShapeDtypeStruct(terms[0].shape, kind) for kind in (jnp.float32, jnp.bfloat16)],
        [VMEM] * len(terms) + [ANYWHERE] * len(tied),
        bytes_accessed=terms[0].size * 2 * (len(terms) + 3),
    )(*terms, *tied)


def project_kernel(
    own_ref, other_ref, own_kv, other_kv, *refs, chunks, block
):
    keep_ref, send_ref = refs[-2:]
    place = my_place()
    kv_t = jnp.concatenate([own_kv[...].T, other_kv[...].T], axis=1)
    half = len(chunks) // 2
    for index, offsets in enumerate(chunks):
        own_start, other_start = chunk_starts(place, offsets, block)
        acts = jnp.concatenate(
            [own_ref[:, pl.ds(own_start, block)], other_ref[:, pl.ds(other_start, block)]], axis=0
        )
        part = jnp.dot(kv_t, acts, preferred_element_type=jnp.float32)
        out_ref = keep_ref if index < half else send_ref
        out_ref[:, pl.ds(index % half * block, block)] = part.astype(out_ref.dtype)


def project(own, other, kvs, tied, chunks, block):
    rows, width = kvs[0].shape
    kept = len(chunks) // 2 * block
    return local_call(
        functools.partial(project_kernel, chunks=chunks, block=block),
        "project",
        [
            jax.ShapeDtypeStruct((width, kept), jnp.float32),
            jax.ShapeDtypeStruct((width, kept), jnp.bfloat16),
        ],
        [VMEM] * 4 + [ANYWHERE] * len(tied),
        flops=8 * rows * width * kept,
        bytes_accessed=4 * rows * kept,
    )(own, other, *kvs, *tied)


def combine_kernel(own_ref, other_ref, *refs, tied, axis):
    out_refs = refs[tied:]
    size = out_refs[0].shape[axis]
    for step, out_ref in enumerate(out_refs):
        part = pl.ds(step * size, size)
        at = (part, slice(None)) if axis == 0 else (slice(None), part)
        total = own_ref[at] + other_ref[at].astype(jnp.float32)
        out_ref[...] = total.astype(out_ref.dtype)


def combine(own, other, types, axis, tied=()):
    shape = list(own.shape)
    shape[axis] //= len(types)
    return local_call(
        functools.partial(combine_kernel, tied=len(tied), axis=axis),
        "combine",
        [jax.ShapeDtypeStruct(tuple(shape), kind) for kind in types],
        [VMEM] * 2 + [ANYWHERE] * len(tied),
        bytes_accessed=8 * own.size,
    )(own, other, *tied)


def lamb_kernel(*refs, planes):
    grad_refs = refs[:planes]
    weight_ref, one_ref, two_ref = refs[planes : planes + 3]
    new_one_ref, new_two_ref, update_ref, sums_ref = refs[planes + 3 :]
    total = grad_refs[0][...]
    for ref in grad_refs[1:]:
        total = total + ref[...].astype(jnp.float32)
    gradient = total.T
    head_dim = weight_ref.shape[2]
    lane = lax.broadcasted_iota(jnp.int32, sums_ref.shape[1:], 1)
    sums = jnp.zeros(sums_ref.shape[1:], jnp.float32)
    for which in range(2):
        grad = gradient[:, which * head_dim : (which + 1) * head_dim]
        weight = weight_ref[which]
        new_one = beta_one * one_ref[which] + (1.0 - beta_one) * grad
        new_two = beta_two * two_ref[which] + (1.0 - beta_two) * grad * grad
        update = new_one / (jnp.sqrt(new_two) + epsilon) + weight_decay * weight
        new_one_ref[which] = new_one
        new_two_ref[which] = new_two
        update_ref[which] = update
        sums = sums + jnp.where(lane == which, jnp.sum(weight * weight), 0.0)
        sums = sums + jnp.where(lane == 2 + which, jnp.sum(update * update), 0.0)
    sums_ref[...] = jnp.broadcast_to(sums[None], sums_ref.shape)


def lamb(gradients, weight, one, two, total):
    state = jax.ShapeDtypeStruct(weight.shape, jnp.float32)
    return local_call(
        functools.partial(lamb_kernel, planes=len(gradients)),
        "lamb",
        [state, state, state, jax.ShapeDtypeStruct((total, 8, 128), jnp.float32)],
        [VMEM] * (len(gradients) + 3),
        bytes_accessed=28 * weight.size,
    )(*gradients, weight, one, two)


def finish_kernel(sums_ref, weight_ref, update_ref, new_weight_ref, ratio_ref):
    sums = jnp.sum(sums_ref[...], axis=0)[0:1, :]
    lane = lax.broadcasted_iota(jnp.int32, sums.shape, 1)

    def pick(which):
        return jnp.sum(jnp.where(lane == which, sums, 0.0), axis=1, keepdims=True)

    for which in range(2):
        ratio = jnp.sqrt(pick(which)) / (jnp.sqrt(pick(2 + which)) + epsilon)
        new_weight_ref[which] = weight_ref[which] - learn_rate * ratio * update_ref[which]
        ratio_ref[which] = ratio[0, 0]


def finish(sums, weight, update):
    return local_call(
        finish_kernel,
        "finish",
        [
            jax.ShapeDtypeStruct(weight.shape, jnp.float32),
            jax.ShapeDtypeStruct((2,), jnp.float32),
        ],
        [VMEM] * 3,
        out_specs=[VMEM, SMEM],
        bytes_accessed=12 * weight.size,
    )(sums, weight, update)


def on_device_small(
    queries,
    key_states,
    value_states,
    attn_out,
    out_grad,
    activations,
    segment_ids,
    span_order,
    kv_weight,
    moment_one,
    moment_two,
):
    core, up, across = 1, 2, lax.axis_size("dp")
    planes = lax.axis_size("plane")
    places = lax.axis_size("across") * across
    total = planes * places
    count = total // across
    heads = queries.shape[2] // key_states.shape[2]
    block = kv_weight.shape[1]
    keys, values = key_states[0], value_states[0]
    low, full = jnp.bfloat16, jnp.float32

    own, acts = pack(keys, values, segment_ids, activations[0], block)
    other_acts = xor_permute(acts, up, total)
    level = [own] + [xor_permute(own, m * places, total) for m in range(1, planes)]
    passed = [xor_permute(piece, across, total) for piece in level]
    piece, *prepared = prepare(
        span_order, keys, values, segment_ids, queries[0], attn_out[0], out_grad[0], heads, count
    )
    pieces = [piece for pair in zip([piece] + level[1:], passed) for piece in pair]

    probs_t, grads_t, k_t = attention(prepared, pieces, heads)
    squares = (probs_t, grads_t, prepared[0], prepared[1])
    rows = keys.shape[0]
    sent, after = {}, []
    for step in reversed(range(planes)):
        after = kv_terms(*squares, after, [[2 * step + 1]], low, rows)
        [sent[step]] = after
    kept = kv_terms(*squares, after, [[2 * step] for step in range(planes)], full, rows)
    query_grad, mark = query_gradient(k_t, grads_t, heads)
    terms = []
    for step in range(planes):
        kind = full if step == 0 else low
        terms += combine(kept[step], xor_permute(sent[step], across, total), [kind], 0)
    terms = [terms[0]] + [xor_permute(terms[m], m * places, total) for m in range(1, planes)]
    kv_sum, kv_sent = total_kv(terms, [other_acts, mark])
    kv_low = kv_sum.astype(low)

    kvs = [kv_sent, xor_permute(kv_sent, up, total)]
    blocks, after = {}, []
    for group in chunk_groups(planes):
        step = group[0][2]
        keep, send = project(activations[0], other_acts, kvs, [], group, block)
        keep, send = combine(keep, xor_permute(send, core, total), [full, low], 1, after)
        after = [send]
        if step == planes // 2:
            after = [send, blocks[planes - 1]]
        kind = full if step == 0 else low
        [blocks[step]] = combine(keep, xor_permute(send, across, total), [kind], 1)
    gradients = [blocks[0]] + [xor_permute(blocks[m], m * places, total) for m in range(1, planes)]
    new_one, new_two, update, sums = lamb(gradients, kv_weight, moment_one, moment_two, total)
    sums = lax.all_to_all(sums, AXES, split_axis=0, concat_axis=0)
    new_weight, ratios = finish(sums, kv_weight, update)
    return (query_grad[None], kv_low[None], new_weight, new_one, new_two, ratios)


def layout_positions(span_order, first_row, row_count, half):
    layout = first_row + jnp.arange(row_count, dtype=jnp.int32)
    which = layout // half
    table = jnp.arange(span_order.shape[0], dtype=jnp.int32)
    picked = jnp.sum(jnp.where(which[:, None] == table[None, :], span_order[None, :], 0), axis=1)
    return picked * half + layout % half


def block_size(total_rows, query_rows):
    block_rows = total_rows
    while block_rows > 4 * query_rows and block_rows % 2 == 0:
        block_rows = block_rows // 2
    return block_rows


def on_device(
    queries,
    key_states,
    value_states,
    attn_out,
    out_grad,
    activations,
    segment_ids,
    span_order,
    kv_weight,
    moment_one,
    moment_two,
):
    device = lax.axis_index("context")
    query_rows = queries.shape[1]
    half = query_rows // 2
    head_dim = key_states.shape[2]
    heads = queries.shape[2] // head_dim
    score_scale = head_dim ** (-0.5)
    query_heads = queries[0].reshape(query_rows, heads, head_dim)
    grad_heads = out_grad[0].reshape(query_rows, heads, head_dim)
    output_heads = attn_out[0].reshape(query_rows, heads, head_dim)
    delta = jnp.sum(grad_heads.astype(jnp.float32) * output_heads.astype(jnp.float32), axis=2)
    query_place = layout_positions(span_order, device * query_rows, query_rows, half)
    query_segment = segment_ids[0]
    all_segments = lax.all_gather(segment_ids, "context", axis=1, tiled=True)[0]

    def visible_for(first_row, row_count):
        key_place = layout_positions(span_order, first_row, row_count, half)
        key_segment = lax.dynamic_slice_in_dim(all_segments, first_row, row_count, 0)
        visible = (key_place[None, :] <= query_place[:, None]) & (
            key_segment[None, :] == query_segment[:, None]
        )
        return visible[:, None, :]

    def score_block(key_block):
        return (
            jnp.einsum("qhd,kd->qhk", query_heads, key_block, preferred_element_type=jnp.float32)
            * score_scale
        )

    seq_length = query_rows * lax.axis_size("context")
    start_stats = (
        jnp.full((query_rows, heads), -1e30, jnp.float32),
        jnp.zeros((query_rows, heads), jnp.float32),
    )
    start_grads = (
        jnp.zeros((query_rows, heads, head_dim), jnp.float32),
        jnp.zeros((seq_length, 2 * head_dim), jnp.float32),
    )
    key_piece = lax.all_gather(key_states, "context", axis=1, tiled=True)
    value_piece = lax.all_gather(value_states, "context", axis=1, tiled=True)
    piece_rows = key_piece.shape[1]
    block_rows = block_size(piece_rows, query_rows)

    def stats_step(block_index, state):
        row_top, row_total = state
        offset = block_index * block_rows
        key_block = lax.dynamic_slice_in_dim(key_piece[0], offset, block_rows, 0)
        visible = visible_for(offset, block_rows)
        scores = score_block(key_block)
        masked = jnp.where(visible, scores, -1e30)
        new_top = jnp.maximum(row_top, jnp.max(masked, axis=2))
        weights = jnp.where(visible, jnp.exp(scores - new_top[:, :, None]), 0.0)
        return (new_top, row_total * jnp.exp(row_top - new_top) + jnp.sum(weights, axis=2))

    row_top, row_total = lax.fori_loop(0, piece_rows // block_rows, stats_step, start_stats)
    log_total = row_top + jnp.log(row_total)

    def grad_step(block_index, state):
        query_acc, kv_acc = state
        offset = block_index * block_rows
        key_block = lax.dynamic_slice_in_dim(key_piece[0], offset, block_rows, 0)
        value_block = lax.dynamic_slice_in_dim(value_piece[0], offset, block_rows, 0)
        visible = visible_for(offset, block_rows)
        probs = jnp.where(visible, jnp.exp(score_block(key_block) - log_total[:, :, None]), 0.0)
        prob_grad = jnp.einsum(
            "qhd,kd->qhk", grad_heads, value_block, preferred_element_type=jnp.float32
        )
        score_grad = (score_scale * probs * (prob_grad - delta[:, :, None])).astype(jnp.bfloat16)
        query_acc = query_acc + jnp.einsum(
            "qhk,kd->qhd", score_grad, key_block, preferred_element_type=jnp.float32
        )
        key_grad = jnp.einsum(
            "qhk,qhd->kd", score_grad, query_heads, preferred_element_type=jnp.float32
        )
        value_grad = jnp.einsum(
            "qhk,qhd->kd",
            probs.astype(jnp.bfloat16),
            grad_heads,
            preferred_element_type=jnp.float32,
        )
        current = lax.dynamic_slice_in_dim(kv_acc, offset, block_rows, 0)
        summed = current + jnp.concatenate([key_grad, value_grad], axis=1)
        return (query_acc, lax.dynamic_update_slice_in_dim(kv_acc, summed, offset, 0))

    query_acc, kv_acc = lax.fori_loop(0, piece_rows // block_rows, grad_step, start_grads)
    kv_summed = lax.psum_scatter(kv_acc, "context", scatter_dimension=0, tiled=True)
    kv_low = kv_summed.astype(jnp.bfloat16)
    feature_rows = activations[0]
    gradient = lax.psum_scatter(
        lax.dot_general(
            feature_rows, kv_low, (((0,), (0,)), ((), ())), preferred_element_type=jnp.float32
        ),
        ("context", "dp"),
        scatter_dimension=0,
        tiled=True,
    )
    gradient = jnp.stack([gradient[:, :head_dim], gradient[:, head_dim:]])
    new_one = beta_one * moment_one + (1.0 - beta_one) * gradient
    new_two = beta_two * moment_two + (1.0 - beta_two) * gradient * gradient
    update = new_one / (jnp.sqrt(new_two) + epsilon) + weight_decay * kv_weight
    weight_sums, update_sums = lax.psum(
        (jnp.sum(kv_weight * kv_weight, axis=(1, 2)), jnp.sum(update * update, axis=(1, 2))),
        ("context", "dp"),
    )
    trust_ratio = jnp.sqrt(weight_sums) / (jnp.sqrt(update_sums) + epsilon)
    new_weight = kv_weight - learn_rate * trust_ratio[:, None, None] * update
    query_grad = query_acc.reshape(query_rows, heads * head_dim).astype(jnp.bfloat16)
    return (query_grad[None], kv_low[None], new_weight, new_one, new_two, trust_ratio)


def solution(mesh):
    in_specs = (
        P("dp", "context", None),
        P("dp", "context", None),
        P("dp", "context", None),
        P("dp", "context", None),
        P("dp", "context", None),
        P("dp", "context", None),
        P("dp", "context"),
        P(),
        P(None, ("context", "dp"), None),
        P(None, ("context", "dp"), None),
        P(None, ("context", "dp"), None),
    )
    out_specs = (
        P("dp", "context", None),
        P("dp", "context", None),
        P(None, ("context", "dp"), None),
        P(None, ("context", "dp"), None),
        P(None, ("context", "dp"), None),
        P(),
    )
    if mesh.shape["context"] == 8 and mesh.shape["dp"] == 4:
        split = jax.sharding.Mesh(mesh.devices.reshape(4, 2, 4), AXES)
        context = AXES[:2]

        def renamed(specs):
            return tuple(
                P(*[
                    context if name == "context" else AXES if isinstance(name, tuple) else name
                    for name in spec
                ])
                for spec in specs
            )

        return jax.shard_map(
            on_device_small,
            mesh=split,
            in_specs=renamed(in_specs),
            out_specs=renamed(out_specs),
            check_vma=False,
        )
    return jax.shard_map(
        on_device, mesh=mesh, in_specs=in_specs, out_specs=out_specs, check_vma=False
    )
```

```python
import functools

import jax
import jax.numpy as jnp
from jax import lax
from jax.experimental import pallas as pl
from jax.experimental.pallas import tpu as pltpu
from jax.sharding import PartitionSpec as P

beta_one = 0.9
beta_two = 0.999
epsilon = 1e-06
weight_decay = 0.01
learn_rate = 0.01
LOG2E = 1.4426950408889634
VMEM_LIMIT = 40 * 1024 * 1024
VMEM_MOST = 60 * 1024 * 1024
HIDDEN = -1e30
ID_ROWS = 16


AXES = ("plane", "across", "dp")


def my_place():
    dp = lax.axis_index("dp")
    return lax.axis_index("plane"), lax.axis_index("across"), dp // 2, dp % 2


def xor_permute(value, offset, total):
    return lax.ppermute(value, AXES, [(i, i ^ offset) for i in range(total)])


def local_call(kernel, name, out_shape, in_specs, scratch=(), out_specs=None, limit=None, **cost):
    vmem = pl.BlockSpec(memory_space=pltpu.VMEM)
    return pl.pallas_call(
        kernel,
        out_shape=out_shape,
        in_specs=in_specs,
        out_specs=[vmem] * len(out_shape) if out_specs is None else out_specs,
        scratch_shapes=list(scratch),
        compiler_params=pltpu.CompilerParams(vmem_limit_bytes=limit or VMEM_LIMIT),
        cost_estimate=pl.CostEstimate(
            flops=cost.get("flops", 0),
            bytes_accessed=cost.get("bytes_accessed", 0),
            transcendentals=cost.get("transcendentals", 0),
        ),
        name=name,
    )


VMEM = pl.BlockSpec(memory_space=pltpu.VMEM)
SMEM = pl.BlockSpec(memory_space=pltpu.SMEM)
ANYWHERE = pl.BlockSpec(memory_space=pl.ANY)


def write_piece(key_ref, value_ref, ids_ref, out_ref):
    rows, head_dim = key_ref.shape
    out_ref[:rows, :head_dim] = key_ref[...]
    out_ref[:rows, head_dim:] = value_ref[...]
    ids = ids_ref[...].astype(jnp.float32).astype(jnp.bfloat16)
    out_ref[rows:, :rows] = jnp.broadcast_to(ids, (ID_ROWS, rows))
    out_ref[rows:, rows:] = jnp.zeros((ID_ROWS, 2 * head_dim - rows), jnp.bfloat16)


def pack_kernel(
    key_ref, value_ref, ids_ref, act_ref, out_ref, sent_ref, piece, ids, stage, sems, *, block
):
    rows, head_dim = key_ref.shape
    wide = 2 * block
    count = sent_ref.shape[1] // wide
    other = 1 - my_place()[2]
    small = [
        pltpu.make_async_copy(key_ref, piece.at[:rows, :head_dim], sems.at[2 * count]),
        pltpu.make_async_copy(value_ref, piece.at[:rows, head_dim:], sems.at[2 * count + 1]),
        pltpu.make_async_copy(ids_ref, ids, sems.at[2 * count + 2]),
    ]
    arriving, leaving = [], []
    for index in range(count):
        start = pl.multiple_of((2 * index + other) * wide, wide)
        to = pl.ds(index * wide, wide)
        arriving.append(
            pltpu.make_async_copy(
                act_ref.at[:, pl.ds(start, wide)], stage.at[:, to], sems.at[index]
            )
        )
        leaving.append(
            pltpu.make_async_copy(stage.at[:, to], sent_ref.at[:, to], sems.at[count + index])
        )
    for copy in small + arriving:
        copy.start()
    for copy in small:
        copy.wait()
    low = ids[...].astype(jnp.float32).astype(jnp.bfloat16)
    piece[rows:, :rows] = jnp.broadcast_to(low, (ID_ROWS, rows))
    piece[rows:, rows:] = jnp.zeros((ID_ROWS, 2 * head_dim - rows), jnp.bfloat16)
    result = pltpu.make_async_copy(piece, out_ref, sems.at[2 * count + 3])
    result.start()
    for here, there in zip(arriving, leaving):
        here.wait()
        there.start()
    for copy in leaving:
        copy.wait()
    result.wait()


def pack(keys, values, ids, activations, block):
    rows, head_dim = keys.shape
    half = activations.shape[1] // 2
    packed = (rows + ID_ROWS, 2 * head_dim)
    return local_call(
        functools.partial(pack_kernel, block=block),
        "pack",
        [
            jax.ShapeDtypeStruct(packed, jnp.bfloat16),
            jax.ShapeDtypeStruct((rows, half), jnp.bfloat16),
        ],
        [ANYWHERE] * 4,
        [
            pltpu.VMEM(packed, jnp.bfloat16),
            pltpu.VMEM(ids.shape, jnp.int32),
            pltpu.VMEM((rows, half), jnp.bfloat16),
            pltpu.SemaphoreType.DMA((half // block + 4,)),
        ],
        out_specs=[ANYWHERE] * 2,
        limit=VMEM_MOST,
        bytes_accessed=4 * rows * half,
    )(keys, values, ids, activations)


def prepare_kernel(
    span_ref,
    key_ref,
    value_ref,
    ids_ref,
    q_ref,
    o_ref,
    g_ref,
    piece_ref,
    q_all,
    g_all,
    delta_ref,
    base_ref,
    *,
    heads,
    half,
):
    write_piece(key_ref, value_ref, ids_ref, piece_ref)
    rows = q_ref.shape[0]
    head_dim = q_ref.shape[1] // heads
    plane, across, _, _ = my_place()
    me = 2 * plane + across
    for head in range(heads):
        cols = slice(head * head_dim, (head + 1) * head_dim)
        at = pl.ds(head * rows, rows)
        grad = g_ref[:, cols]
        q_all[at, :] = q_ref[:, cols]
        g_all[at, :] = grad
        product = grad.astype(jnp.float32) * o_ref[:, cols].astype(jnp.float32)
        delta_ref[:, at] = jnp.sum(product.T, axis=0, keepdims=True)
    for piece in range(base_ref.shape[0] // 2):
        for part in range(2):
            start = span_ref[2 * (me ^ piece) + part] * half
            base_ref[2 * piece + part : 2 * piece + part + 1, :] = jnp.full(
                (1, rows), start, jnp.int32
            )


def prepare(span_order, keys, values, ids, queries, attn_out, out_grad, heads, count):
    rows, width = queries.shape
    head_dim = width // heads
    stacked = jax.ShapeDtypeStruct((heads * rows, head_dim), jnp.bfloat16)
    return local_call(
        functools.partial(prepare_kernel, heads=heads, half=rows // 2),
        "prepare_queries",
        [
            jax.ShapeDtypeStruct((rows + ID_ROWS, 2 * head_dim), jnp.bfloat16),
            stacked,
            stacked,
            jax.ShapeDtypeStruct((1, heads * rows), jnp.float32),
            jax.ShapeDtypeStruct((2 * count, rows), jnp.int32),
        ],
        [SMEM] + [VMEM] * 6,
        flops=2 * rows * width,
        bytes_accessed=10 * rows * width,
    )(span_order, keys, values, ids, queries, attn_out, out_grad)


def attention_kernel(q_all, g_all, delta_ref, base_ref, *refs, pieces, heads):
    piece_refs = refs[:pieces]
    probs_t, grads_t, k_t, k_all, v_all, bias = refs[pieces:]
    head_dim = q_all.shape[1]
    rows = q_all.shape[0] // heads
    half = rows // 2
    score_scale = head_dim ** (-0.5)

    for piece in range(pieces):
        at = pl.ds(piece * rows, rows)
        key = piece_refs[piece][:rows, :head_dim]
        k_all[at, :] = key
        v_all[at, :] = piece_refs[piece][:rows, head_dim:]
        k_t[:, at] = key.T

    segment_rows = [
        piece_refs[piece][rows : rows + 1, :rows].astype(jnp.float32) for piece in range(pieces)
    ]
    all_segments = jnp.concatenate(segment_rows, axis=0)
    mine = segment_rows[0]
    first = jnp.zeros((1, rows), jnp.int32)
    for document in range(1, 4):
        before = jnp.sum((all_segments < document).astype(jnp.int32))
        first = jnp.where(mine >= document, before, first)
    lane = lax.broadcasted_iota(jnp.int32, (1, rows), 1)
    place = jnp.where(lane < half, base_ref[0:1, :] + lane, base_ref[1:2, :] + lane - half)
    step = lax.broadcasted_iota(jnp.int32, (half, rows), 0)
    for part in range(2 * pieces):
        key_place = base_ref[part : part + 1, :] + step
        visible = (key_place >= first) & (key_place <= place)
        bias[pl.ds(part * half, half), :] = jnp.where(visible, 0.0, HIDDEN)

    group = 2
    width = group * rows
    for start in range(0, heads, group):
        at = pl.ds(start * rows, width)
        contract = (((1,), (1,)), ((), ()))
        scores = lax.dot_general(
            k_all[...], q_all[at, :], contract, preferred_element_type=jnp.float32
        )
        blocked = bias[...]
        scores = scores * (score_scale * LOG2E) + jnp.concatenate([blocked] * group, axis=1)
        top = jnp.max(scores, axis=0, keepdims=True)
        weights = jnp.exp2(scores - top)
        probs = weights * (1.0 / jnp.sum(weights, axis=0, keepdims=True))
        probs_t[:, at] = probs.astype(jnp.bfloat16)
        prob_grad = lax.dot_general(
            v_all[...], g_all[at, :], contract, preferred_element_type=jnp.float32
        )
        grads_t[:, at] = (score_scale * probs * (prob_grad - delta_ref[:, at])).astype(jnp.bfloat16)


def attention(prepared, pieces, heads):
    stacked, head_dim = prepared[0].shape
    rows = stacked // heads
    keys = len(pieces) * rows
    work = stacked * keys
    square = jax.ShapeDtypeStruct((keys, stacked), jnp.bfloat16)
    return local_call(
        functools.partial(attention_kernel, pieces=len(pieces), heads=heads),
        "attention_scores",
        [square, square, jax.ShapeDtypeStruct((head_dim, keys), jnp.bfloat16)],
        [VMEM] * (4 + len(pieces)),
        [
            pltpu.VMEM((keys, head_dim), jnp.bfloat16),
            pltpu.VMEM((keys, head_dim), jnp.bfloat16),
            pltpu.VMEM((keys, rows), jnp.float32),
        ],
        flops=4 * work * head_dim,
        bytes_accessed=4 * work,
        transcendentals=work,
    )(*prepared, *pieces)


def terms_kernel(probs_t, grads_t, q_all, g_all, *refs, groups, rows):
    out_refs = refs[-len(groups) :]
    head_dim = q_all.shape[1]
    for out_ref, group in zip(out_refs, groups):
        for index, piece in enumerate(group):
            at = pl.ds(piece * rows, rows)
            to = pl.ds(index * rows, rows)
            key_grad = jnp.dot(grads_t[at, :], q_all[...], preferred_element_type=jnp.float32)
            value_grad = jnp.dot(probs_t[at, :], g_all[...], preferred_element_type=jnp.float32)
            out_ref[to, :head_dim] = key_grad.astype(out_ref.dtype)
            out_ref[to, head_dim:] = value_grad.astype(out_ref.dtype)


def kv_terms(probs_t, grads_t, q_all, g_all, tied, groups, kind, rows):
    keys, stacked = probs_t.shape
    head_dim = q_all.shape[1]
    return local_call(
        functools.partial(terms_kernel, groups=groups, rows=rows),
        "kv_terms",
        [jax.ShapeDtypeStruct((len(group) * rows, 2 * head_dim), kind) for group in groups],
        [VMEM] * 4 + [ANYWHERE] * len(tied),
        flops=2 * keys * stacked * head_dim,
        bytes_accessed=2 * keys * stacked,
    )(probs_t, grads_t, q_all, g_all, *tied)


def query_kernel(k_t, grads_t, dq_ref, mark_ref, *, heads):
    mark_ref[...] = jnp.zeros_like(mark_ref)
    head_dim = k_t.shape[0]
    rows = grads_t.shape[1] // heads
    group = 2
    for start in range(0, heads, group):
        at = pl.ds(start * rows, group * rows)
        query_t = jnp.dot(k_t[...], grads_t[:, at], preferred_element_type=jnp.float32)
        for head in range(group):
            block = query_t[:, head * rows : (head + 1) * rows].T
            cols = pl.ds((start + head) * head_dim, head_dim)
            dq_ref[:, cols] = block.astype(jnp.bfloat16)


def query_gradient(k_t, grads_t, heads):
    head_dim, keys = k_t.shape
    stacked = grads_t.shape[1]
    return local_call(
        functools.partial(query_kernel, heads=heads),
        "query_gradient",
        [
            jax.ShapeDtypeStruct((stacked // heads, heads * head_dim), jnp.bfloat16),
            jax.ShapeDtypeStruct((8, 128), jnp.float32),
        ],
        [VMEM] * 2,
        flops=2 * keys * stacked * head_dim,
        bytes_accessed=2 * keys * stacked,
    )(k_t, grads_t)


def chunk_groups(planes):
    return [
        [(core, across, step) for core in range(2) for across in range(2)]
        for step in reversed(range(planes))
    ]


def chunk_starts(place, offsets, block):
    core, across, step = offsets
    chip = (place[0] ^ step) * 2 + (place[1] ^ across)
    core = place[3] ^ core
    own = ((2 * chip + place[2]) * 2 + core) * block
    return pl.multiple_of(own, block), pl.multiple_of((2 * chip + core) * block, block)


def total_kernel(*refs, count):
    total = refs[0][...]
    for ref in refs[1:count]:
        total = total + ref[...].astype(jnp.float32)
    refs[-2][...] = total
    refs[-1][...] = total.astype(jnp.bfloat16)


def total_kv(terms, tied):
    return local_call(
        functools.partial(total_kernel, count=len(terms)),
        "total_kv",
        [jax.ShapeDtypeStruct(terms[0].shape, kind) for kind in (jnp.float32, jnp.bfloat16)],
        [VMEM] * len(terms) + [ANYWHERE] * len(tied),
        bytes_accessed=terms[0].size * 2 * (len(terms) + 3),
    )(*terms, *tied)


def project_kernel(
    own_ref, other_ref, own_kv, other_kv, *refs, chunks, block
):
    keep_ref, send_ref = refs[-2:]
    place = my_place()
    kv_t = jnp.concatenate([own_kv[...].T, other_kv[...].T], axis=1)
    half = len(chunks) // 2
    for index, offsets in enumerate(chunks):
        own_start, other_start = chunk_starts(place, offsets, block)
        acts = jnp.concatenate(
            [own_ref[:, pl.ds(own_start, block)], other_ref[:, pl.ds(other_start, block)]], axis=0
        )
        part = jnp.dot(kv_t, acts, preferred_element_type=jnp.float32)
        out_ref = keep_ref if index < half else send_ref
        out_ref[:, pl.ds(index % half * block, block)] = part.astype(out_ref.dtype)


def project(own, other, kvs, tied, chunks, block):
    rows, width = kvs[0].shape
    kept = len(chunks) // 2 * block
    return local_call(
        functools.partial(project_kernel, chunks=chunks, block=block),
        "project",
        [
            jax.ShapeDtypeStruct((width, kept), jnp.float32),
            jax.ShapeDtypeStruct((width, kept), jnp.bfloat16),
        ],
        [VMEM] * 4 + [ANYWHERE] * len(tied),
        flops=8 * rows * width * kept,
        bytes_accessed=4 * rows * kept,
    )(own, other, *kvs, *tied)


def combine_kernel(own_ref, other_ref, *refs, tied, axis):
    out_refs = refs[tied:]
    size = out_refs[0].shape[axis]
    for step, out_ref in enumerate(out_refs):
        part = pl.ds(step * size, size)
        at = (part, slice(None)) if axis == 0 else (slice(None), part)
        total = own_ref[at] + other_ref[at].astype(jnp.float32)
        out_ref[...] = total.astype(out_ref.dtype)


def combine(own, other, types, axis, tied=()):
    shape = list(own.shape)
    shape[axis] //= len(types)
    return local_call(
        functools.partial(combine_kernel, tied=len(tied), axis=axis),
        "combine",
        [jax.ShapeDtypeStruct(tuple(shape), kind) for kind in types],
        [VMEM] * 2 + [ANYWHERE] * len(tied),
        bytes_accessed=8 * own.size,
    )(own, other, *tied)


def lamb_kernel(*refs, planes):
    grad_refs = refs[:planes]
    weight_ref, one_ref, two_ref = refs[planes : planes + 3]
    new_one_ref, new_two_ref, update_ref, sums_ref = refs[planes + 3 :]
    total = grad_refs[0][...]
    for ref in grad_refs[1:]:
        total = total + ref[...].astype(jnp.float32)
    gradient = total.T
    head_dim = weight_ref.shape[2]
    lane = lax.broadcasted_iota(jnp.int32, sums_ref.shape[1:], 1)
    sums = jnp.zeros(sums_ref.shape[1:], jnp.float32)
    for which in range(2):
        grad = gradient[:, which * head_dim : (which + 1) * head_dim]
        weight = weight_ref[which]
        new_one = beta_one * one_ref[which] + (1.0 - beta_one) * grad
        new_two = beta_two * two_ref[which] + (1.0 - beta_two) * grad * grad
        update = new_one / (jnp.sqrt(new_two) + epsilon) + weight_decay * weight
        new_one_ref[which] = new_one
        new_two_ref[which] = new_two
        update_ref[which] = update
        sums = sums + jnp.where(lane == which, jnp.sum(weight * weight), 0.0)
        sums = sums + jnp.where(lane == 2 + which, jnp.sum(update * update), 0.0)
    sums_ref[...] = jnp.broadcast_to(sums[None], sums_ref.shape)


def lamb(gradients, weight, one, two, total):
    state = jax.ShapeDtypeStruct(weight.shape, jnp.float32)
    return local_call(
        functools.partial(lamb_kernel, planes=len(gradients)),
        "lamb",
        [state, state, state, jax.ShapeDtypeStruct((total, 8, 128), jnp.float32)],
        [VMEM] * (len(gradients) + 3),
        bytes_accessed=28 * weight.size,
    )(*gradients, weight, one, two)


def finish_kernel(sums_ref, weight_ref, update_ref, new_weight_ref, ratio_ref):
    sums = jnp.sum(sums_ref[...], axis=0)[0:1, :]
    lane = lax.broadcasted_iota(jnp.int32, sums.shape, 1)

    def pick(which):
        return jnp.sum(jnp.where(lane == which, sums, 0.0), axis=1, keepdims=True)

    for which in range(2):
        ratio = jnp.sqrt(pick(which)) / (jnp.sqrt(pick(2 + which)) + epsilon)
        new_weight_ref[which] = weight_ref[which] - learn_rate * ratio * update_ref[which]
        ratio_ref[which] = ratio[0, 0]


def finish(sums, weight, update):
    return local_call(
        finish_kernel,
        "finish",
        [
            jax.ShapeDtypeStruct(weight.shape, jnp.float32),
            jax.ShapeDtypeStruct((2,), jnp.float32),
        ],
        [VMEM] * 3,
        out_specs=[VMEM, SMEM],
        bytes_accessed=12 * weight.size,
    )(sums, weight, update)


def on_device_small(
    queries,
    key_states,
    value_states,
    attn_out,
    out_grad,
    activations,
    segment_ids,
    span_order,
    kv_weight,
    moment_one,
    moment_two,
):
    core, up, across = 1, 2, lax.axis_size("dp")
    planes = lax.axis_size("plane")
    places = lax.axis_size("across") * across
    total = planes * places
    count = total // across
    heads = queries.shape[2] // key_states.shape[2]
    block = kv_weight.shape[1]
    keys, values = key_states[0], value_states[0]
    low, full = jnp.bfloat16, jnp.float32

    own, acts = pack(keys, values, segment_ids, activations[0], block)
    other_acts = xor_permute(acts, up, total)
    level = [own] + [xor_permute(own, m * places, total) for m in range(1, planes)]
    passed = [xor_permute(piece, across, total) for piece in level]
    piece, *prepared = prepare(
        span_order, keys, values, segment_ids, queries[0], attn_out[0], out_grad[0], heads, count
    )
    pieces = [piece for pair in zip([piece] + level[1:], passed) for piece in pair]

    probs_t, grads_t, k_t = attention(prepared, pieces, heads)
    squares = (probs_t, grads_t, prepared[0], prepared[1])
    rows = keys.shape[0]
    sent, after = {}, []
    for step in reversed(range(planes)):
        after = kv_terms(*squares, after, [[2 * step + 1]], low, rows)
        [sent[step]] = after
    kept = kv_terms(*squares, after, [[2 * step] for step in range(planes)], full, rows)
    query_grad, mark = query_gradient(k_t, grads_t, heads)
    terms = []
    for step in range(planes):
        kind = full if step == 0 else low
        terms += combine(kept[step], xor_permute(sent[step], across, total), [kind], 0)
    terms = [terms[0]] + [xor_permute(terms[m], m * places, total) for m in range(1, planes)]
    kv_sum, kv_sent = total_kv(terms, [other_acts, mark])
    kv_low = kv_sum.astype(low)

    kvs = [kv_sent, xor_permute(kv_sent, up, total)]
    blocks, after = {}, []
    for group in chunk_groups(planes):
        step = group[0][2]
        ahead = [blocks[planes - 1]] if step < planes // 2 else []
        keep, send = project(activations[0], other_acts, kvs, ahead, group, block)
        keep, send = combine(keep, xor_permute(send, core, total), [full, low], 1, after)
        after = [send]
        if step == planes // 2:
            after = [send, blocks[planes - 1]]
        kind = full if step == 0 else low
        [blocks[step]] = combine(keep, xor_permute(send, across, total), [kind], 1)
    gradients = [blocks[0]] + [xor_permute(blocks[m], m * places, total) for m in range(1, planes)]
    new_one, new_two, update, sums = lamb(gradients, kv_weight, moment_one, moment_two, total)
    sums = lax.all_to_all(sums, AXES, split_axis=0, concat_axis=0)
    new_weight, ratios = finish(sums, kv_weight, update)
    return (query_grad[None], kv_low[None], new_weight, new_one, new_two, ratios)


def layout_positions(span_order, first_row, row_count, half):
    layout = first_row + jnp.arange(row_count, dtype=jnp.int32)
    which = layout // half
    table = jnp.arange(span_order.shape[0], dtype=jnp.int32)
    picked = jnp.sum(jnp.where(which[:, None] == table[None, :], span_order[None, :], 0), axis=1)
    return picked * half + layout % half


def block_size(total_rows, query_rows):
    block_rows = total_rows
    while block_rows > 4 * query_rows and block_rows % 2 == 0:
        block_rows = block_rows // 2
    return block_rows


def on_device(
    queries,
    key_states,
    value_states,
    attn_out,
    out_grad,
    activations,
    segment_ids,
    span_order,
    kv_weight,
    moment_one,
    moment_two,
):
    device = lax.axis_index("context")
    query_rows = queries.shape[1]
    half = query_rows // 2
    head_dim = key_states.shape[2]
    heads = queries.shape[2] // head_dim
    score_scale = head_dim ** (-0.5)
    query_heads = queries[0].reshape(query_rows, heads, head_dim)
    grad_heads = out_grad[0].reshape(query_rows, heads, head_dim)
    output_heads = attn_out[0].reshape(query_rows, heads, head_dim)
    delta = jnp.sum(grad_heads.astype(jnp.float32) * output_heads.astype(jnp.float32), axis=2)
    query_place = layout_positions(span_order, device * query_rows, query_rows, half)
    query_segment = segment_ids[0]
    all_segments = lax.all_gather(segment_ids, "context", axis=1, tiled=True)[0]

    def visible_for(first_row, row_count):
        key_place = layout_positions(span_order, first_row, row_count, half)
        key_segment = lax.dynamic_slice_in_dim(all_segments, first_row, row_count, 0)
        visible = (key_place[None, :] <= query_place[:, None]) & (
            key_segment[None, :] == query_segment[:, None]
        )
        return visible[:, None, :]

    def score_block(key_block):
        return (
            jnp.einsum("qhd,kd->qhk", query_heads, key_block, preferred_element_type=jnp.float32)
            * score_scale
        )

    seq_length = query_rows * lax.axis_size("context")
    start_stats = (
        jnp.full((query_rows, heads), -1e30, jnp.float32),
        jnp.zeros((query_rows, heads), jnp.float32),
    )
    start_grads = (
        jnp.zeros((query_rows, heads, head_dim), jnp.float32),
        jnp.zeros((seq_length, 2 * head_dim), jnp.float32),
    )
    key_piece = lax.all_gather(key_states, "context", axis=1, tiled=True)
    value_piece = lax.all_gather(value_states, "context", axis=1, tiled=True)
    piece_rows = key_piece.shape[1]
    block_rows = block_size(piece_rows, query_rows)

    def stats_step(block_index, state):
        row_top, row_total = state
        offset = block_index * block_rows
        key_block = lax.dynamic_slice_in_dim(key_piece[0], offset, block_rows, 0)
        visible = visible_for(offset, block_rows)
        scores = score_block(key_block)
        masked = jnp.where(visible, scores, -1e30)
        new_top = jnp.maximum(row_top, jnp.max(masked, axis=2))
        weights = jnp.where(visible, jnp.exp(scores - new_top[:, :, None]), 0.0)
        return (new_top, row_total * jnp.exp(row_top - new_top) + jnp.sum(weights, axis=2))

    row_top, row_total = lax.fori_loop(0, piece_rows // block_rows, stats_step, start_stats)
    log_total = row_top + jnp.log(row_total)

    def grad_step(block_index, state):
        query_acc, kv_acc = state
        offset = block_index * block_rows
        key_block = lax.dynamic_slice_in_dim(key_piece[0], offset, block_rows, 0)
        value_block = lax.dynamic_slice_in_dim(value_piece[0], offset, block_rows, 0)
        visible = visible_for(offset, block_rows)
        probs = jnp.where(visible, jnp.exp(score_block(key_block) - log_total[:, :, None]), 0.0)
        prob_grad = jnp.einsum(
            "qhd,kd->qhk", grad_heads, value_block, preferred_element_type=jnp.float32
        )
        score_grad = (score_scale * probs * (prob_grad - delta[:, :, None])).astype(jnp.bfloat16)
        query_acc = query_acc + jnp.einsum(
            "qhk,kd->qhd", score_grad, key_block, preferred_element_type=jnp.float32
        )
        key_grad = jnp.einsum(
            "qhk,qhd->kd", score_grad, query_heads, preferred_element_type=jnp.float32
        )
        value_grad = jnp.einsum(
            "qhk,qhd->kd",
            probs.astype(jnp.bfloat16),
            grad_heads,
            preferred_element_type=jnp.float32,
        )
        current = lax.dynamic_slice_in_dim(kv_acc, offset, block_rows, 0)
        summed = current + jnp.concatenate([key_grad, value_grad], axis=1)
        return (query_acc, lax.dynamic_update_slice_in_dim(kv_acc, summed, offset, 0))

    query_acc, kv_acc = lax.fori_loop(0, piece_rows // block_rows, grad_step, start_grads)
    kv_summed = lax.psum_scatter(kv_acc, "context", scatter_dimension=0, tiled=True)
    kv_low = kv_summed.astype(jnp.bfloat16)
    feature_rows = activations[0]
    gradient = lax.psum_scatter(
        lax.dot_general(
            feature_rows, kv_low, (((0,), (0,)), ((), ())), preferred_element_type=jnp.float32
        ),
        ("context", "dp"),
        scatter_dimension=0,
        tiled=True,
    )
    gradient = jnp.stack([gradient[:, :head_dim], gradient[:, head_dim:]])
    new_one = beta_one * moment_one + (1.0 - beta_one) * gradient
    new_two = beta_two * moment_two + (1.0 - beta_two) * gradient * gradient
    update = new_one / (jnp.sqrt(new_two) + epsilon) + weight_decay * kv_weight
    weight_sums, update_sums = lax.psum(
        (jnp.sum(kv_weight * kv_weight, axis=(1, 2)), jnp.sum(update * update, axis=(1, 2))),
        ("context", "dp"),
    )
    trust_ratio = jnp.sqrt(weight_sums) / (jnp.sqrt(update_sums) + epsilon)
    new_weight = kv_weight - learn_rate * trust_ratio[:, None, None] * update
    query_grad = query_acc.reshape(query_rows, heads * head_dim).astype(jnp.bfloat16)
    return (query_grad[None], kv_low[None], new_weight, new_one, new_two, trust_ratio)


def solution(mesh):
    in_specs = (
        P("dp", "context", None),
        P("dp", "context", None),
        P("dp", "context", None),
        P("dp", "context", None),
        P("dp", "context", None),
        P("dp", "context", None),
        P("dp", "context"),
        P(),
        P(None, ("context", "dp"), None),
        P(None, ("context", "dp"), None),
        P(None, ("context", "dp"), None),
    )
    out_specs = (
        P("dp", "context", None),
        P("dp", "context", None),
        P(None, ("context", "dp"), None),
        P(None, ("context", "dp"), None),
        P(None, ("context", "dp"), None),
        P(),
    )
    if mesh.shape["context"] == 8 and mesh.shape["dp"] == 4:
        split = jax.sharding.Mesh(mesh.devices.reshape(4, 2, 4), AXES)
        context = AXES[:2]

        def renamed(specs):
            return tuple(
                P(*[
                    context if name == "context" else AXES if isinstance(name, tuple) else name
                    for name in spec
                ])
                for spec in specs
            )

        return jax.shard_map(
            on_device_small,
            mesh=split,
            in_specs=renamed(in_specs),
            out_specs=renamed(out_specs),
            check_vma=False,
        )
    return jax.shard_map(
        on_device, mesh=mesh, in_specs=in_specs, out_specs=out_specs, check_vma=False
    )
```
